256 devices in a mesh: gx: 64 (over z, y, x_lo), gy: 4 (over x_hi, core).
Axes of the slice: x: 4 (x_hi: 2, x_lo: 2; x = x_hi * 2 + x_lo), y: 4, z: 8, core: 2. Of those that a mesh axis runs over, the one named last changes fastest.
Arguments:
- traces: float32 [64, 8, 4, 128, 1024], P('gx', 'gy'), may hold values from -6 to 6
- leaf_maps: float32 [64, 8, 512, 512], P('gx', 'gy'), may hold values from -4 to 16, as said below
- decap_mask: int32 [64, 8, 4, 8], P('gx', 'gy'), may hold values 0 or 1
Outputs:
- box_maps: float32 [64, 8, 256, 256], P('gx', 'gy')
- box_loads: float32 [64, 8, 256, 1024], P('gx', 'gy')
The draws below stay inside these ranges and needn't reach their ends.
Inputs may be any that keep to these rules, and one draw needn't show every extreme that they name: `leaf_maps`: every tile's map is symmetric positive definite.
All inputs are finite; a program needn't handle non-finite values. No bound on the sum of `decap_mask` on one device may be relied on, other than what follows from the above.
Results may differ from the reference program's by a relative error of at most 0.0001.
Values sent between devices are 32-bit elements; how exact they have to be, the bound alone decides.
A program may use at most 64 MiB of HBM per device.

```python
import math
import jax
import jax.numpy as jnp
from jax import lax

E = 128
K = 1024
PB = 16
LEVELS = 3
NXT = 64
NYT = 8


def draw_leaf_maps(key, part):
    first, second = jax.random.split(key, 2)
    ports_all = 4 * E
    shape = (NXT, NYT, ports_all, ports_all)
    raw = jax.random.uniform(first, shape, jnp.float32, -math.sqrt(3.0), math.sqrt(3.0))

    def gram_row(block):
        product = jnp.matmul(block, jnp.swapaxes(block, -1, -2), precision=lax.Precision.HIGHEST) / ports_all
        return 0.5 * (product + jnp.swapaxes(product, -1, -2))
    gram = lax.map(gram_row, raw)
    shifts = 0.05 + 0.1 * jax.random.uniform(second, shape[:-1], jnp.float32)
    maps = gram + shifts[..., None] * jnp.eye(ports_all, dtype=jnp.float32)
    return maps


def touch_ends(array, own_key, least, high):
    longest = array.shape.index(max(array.shape))
    spots = []
    for shift in (0, 1):
        where = [jax.random.randint(jax.random.fold_in(own_key, axis), (), 0, length) for axis, length in enumerate(array.shape)]
        where[longest] = (where[longest] + shift) % array.shape[longest]
        spots.append(tuple(where))
    return array.at[spots[0]].set(least).at[spots[1]].set(high)


def steps_of(stream_key, extent, cuts, smallest, high):
    def one(axis_at, parts):
        steps = jax.random.uniform(jax.random.fold_in(jax.random.fold_in(stream_key, 6), axis_at), (parts,), jnp.float32, smallest / len(cuts), high / len(cuts))
        return jnp.repeat(jnp.exp(steps), extent[axis_at] // parts).reshape((-1,) + (1,) * (len(extent) - axis_at - 1))

    level = one(*cuts[0])
    for cut in cuts[1:]:
        level = level * one(*cut)
    return level


def scatter_about(rng, dims, scale, most, cuts=(), kind=jnp.bfloat16):
    drawn = jax.random.normal(rng, dims, jnp.float32) * scale
    if len(cuts) > 0:
        drawn = steps_of(rng, dims, cuts, -0.22, 0.18) * drawn
    return jnp.clip(drawn, min=-most, max=most).astype(kind)


def setup_inputs(seed: int = 0) -> dict:
    key_list = jax.random.split(jax.random.key(seed), 4)
    return {
        "traces": scatter_about(key_list[0], (NXT, NYT, 4, E, K), 1.0, 6.0, ((0, 64), (1, 4)), jnp.float32),
        "leaf_maps": draw_leaf_maps(jax.random.fold_in(key_list[3], 71), 0),
        "decap_mask": touch_ends((jax.random.randint(key_list[2], (NXT, NYT, 4, E // PB), 0, 2) < 1).astype(jnp.int32), jax.random.fold_in(key_list[2], 1), 0, 1),
    }


decap_admittance = 2.0

def matprod(left, right):
    return jnp.matmul(left, right, precision=lax.Precision.HIGHEST)

def merge_boxes(left_map, left_load, right_map, right_load, edge):
    a_ww = left_map[..., :edge, :edge]
    a_we = left_map[..., :edge, edge:]
    a_ew = left_map[..., edge:, :edge]
    a_ee = left_map[..., edge:, edge:]
    b_ww = right_map[..., :edge, :edge]
    b_we = right_map[..., :edge, edge:]
    b_ew = right_map[..., edge:, :edge]
    b_ee = right_map[..., edge:, edge:]
    inter = a_ee + b_ww
    factor = jnp.linalg.cholesky(inter)
    stacked = jnp.concatenate([a_ew, b_we, left_load[..., edge:, :] + right_load[..., :edge, :]], axis=-1)
    half = jax.scipy.linalg.solve_triangular(factor, stacked, lower=True)
    solved = jax.scipy.linalg.solve_triangular(factor, half, lower=True, trans=1)
    first = solved[..., :edge]
    second = solved[..., edge:2 * edge]
    third = solved[..., 2 * edge:]
    west = jnp.concatenate([a_ww - matprod(a_we, first), -matprod(a_we, second)], axis=-1)
    east = jnp.concatenate([-matprod(b_ew, first), b_ee - matprod(b_ew, second)], axis=-1)
    west_load = left_load[..., :edge, :] - matprod(a_we, third)
    east_load = right_load[..., edge:, :] - matprod(b_ew, third)
    return (jnp.concatenate([west, east], axis=-2), jnp.concatenate([west_load, east_load], axis=-2))

def reference(traces, leaf_maps, decap_mask):
    edge = E
    ports_all = 4 * E
    ports = jnp.repeat(decap_mask.astype(jnp.float32), PB, axis=-1).reshape(NXT, NYT, ports_all)
    maps = leaf_maps + decap_admittance * ports[..., None] * jnp.eye(ports_all, dtype=jnp.float32)
    from_west = jnp.roll(traces[:, :, 1], 1, axis=0)
    from_east = jnp.roll(traces[:, :, 0], -1, axis=0)
    from_south = jnp.roll(traces[:, :, 3], 1, axis=1)
    from_north = jnp.roll(traces[:, :, 2], -1, axis=1)
    neighbour = jnp.stack([from_west, from_east, from_south, from_north], axis=2)
    averaged = 0.5 * (traces + neighbour)

    def leaf_load(pair):
        column_maps, column_traces = pair
        return matprod(column_maps[:, :2 * edge, :], column_traces.reshape(NYT, ports_all, K))
    box_load = lax.map(leaf_load, (maps, averaged))
    box_map = maps[:, :, :2 * edge, :2 * edge]
    for level in range(LEVELS):
        box_map, box_load = merge_boxes(box_map[0::2], box_load[0::2], box_map[1::2], box_load[1::2], edge)
    box_maps = jnp.repeat(box_map, 2 ** LEVELS, axis=0)
    box_loads = jnp.repeat(box_load, 2 ** LEVELS, axis=0)
    return (box_maps, box_loads)
```

```python
import functools

import jax
import jax.numpy as jnp
from jax import lax
from jax.experimental import pallas as pl
from jax.experimental.pallas import tpu as pltpu
from jax.sharding import PartitionSpec as P

E = 128
K = 1024
PB = 16
F32 = jnp.float32
BF16 = jnp.bfloat16
NB = 32
MESH = pl.DeviceIdType.MESH

decap_admittance = 2.0


def exact(left, right):
    return jnp.dot(left, right, precision=lax.Precision.HIGHEST, preferred_element_type=F32)


def halves(a):
    high = a.astype(BF16)
    return high, (a - high.astype(F32)).astype(BF16)


def split_dot(left, right):
    lh, ll = left
    rh, rl = right
    dot = functools.partial(jnp.dot, preferred_element_type=F32)
    return dot(lh, rl) + dot(ll, rh) + dot(lh, rh)


def near(left, right):
    return split_dot(halves(left), halves(right))


def invert_blocks(blocks):
    n = blocks[0].shape[0]
    lane = lax.broadcasted_iota(jnp.int32, (n, n), 1)
    row = lax.broadcasted_iota(jnp.int32, (n, n), 0)
    lane8 = lane[:8]
    for k in range(0, n, 2):
        done = []
        for a in blocks:
            c0 = jnp.broadcast_to(a[:, k : k + 1], (n, n))
            c1 = jnp.broadcast_to(a[:, k + 1 : k + 2], (n, n))

            def spread(v, i):
                return jnp.broadcast_to(v[i : i + 1, :], (8, n))

            inv0 = 1.0 / spread(c0, k)
            ratio = spread(c0, k + 1) * inv0
            inv1 = 1.0 / (spread(c1, k + 1) - ratio * spread(c1, k))
            r0 = jnp.where(lane8 == k, 1.0, jnp.where(lane8 == k + 1, 0.0, spread(a, k)))
            r1 = jnp.where(lane8 == k + 1, 1.0, jnp.where(lane8 == k, 0.0, spread(a, k + 1)))
            y1 = (r1 - ratio * r0) * inv1
            y0 = r0 * inv0 - ratio * y1
            y0 = jnp.broadcast_to(y0[:1], (n, n))
            y1 = jnp.broadcast_to(y1[:1], (n, n))
            new = jnp.where((lane >> 1) == (k >> 1), 0.0, a) - c0 * y0 - c1 * y1
            done.append(jnp.where(row == k, y0, jnp.where(row == k + 1, y1, new)))
        blocks = done
    return blocks


def solve_all(systems, sides):
    n = E
    for p in range(0, n, NB):
        inverses = invert_blocks([s[p : p + NB, p : p + NB] for s in systems])
        next_systems, next_sides = [], []
        for s, r, inverse in zip(systems, sides, inverses):
            last = p + NB == n
            full = r if last else jnp.concatenate([s[:, p + NB :], r], axis=1)
            pivot = exact(inverse, full[p : p + NB])
            parts = []
            if p:
                parts.append(full[:p] - exact(s[:p, p : p + NB], pivot))
            parts.append(pivot)
            if not last:
                parts.append(full[p + NB :] - exact(s[p + NB :, p : p + NB], pivot))
            full = jnp.concatenate(parts, axis=0)
            if not last:
                rest = n - p - NB
                next_systems.append(jnp.concatenate([jnp.zeros((n, p + NB), F32), full[:, :rest]], axis=1))
                full = full[:, rest:]
            next_sides.append(full)
        systems, sides = next_systems, next_sides
    return sides


def merged(outer_left, outer_right, side, solved):
    across = jnp.transpose(side)
    ww = outer_left - exact(across[:E], solved[:, :E])
    low = exact(across[E:], solved)
    return ww, -low[:, :E], outer_right - low[:, E:]


def kernel(
    size_x, size_y,
    mask, traces, leaf, box_maps, box_loads,
    lm, tv, m0, m1, rx, to, te, tc, tx, xt0, q_hi, q_lo, ps, pr, total, a2, xt1, m2, fin,
    local_sem, early_send, early_recv, m0_send, m0_recv, m1_send, m1_recv,
    pr_send, pr_recv, a2_send, a2_recv, fin_send, fin_recv,
):
    gx = lax.axis_index("gx")
    gy = lax.axis_index("gy")
    x = lax.rem(gx, 2)
    y = lax.rem(lax.div(gx, 2), 4)
    base = gx - lax.rem(gx, 8)
    core = lax.rem(gy, 2)
    partner = (gx + 1 - 2 * x, gy)
    back = lax.rem(gx + size_x - 2, size_x)
    ahead = lax.rem(gx + 2, size_x)
    on_chip = (gx, gy + 1 - 2 * core)
    off_chip = (gx + 1 - 2 * x, lax.rem(gy + size_y + 2 * core - 1, size_y))
    outward = (back + x * (ahead - back), gy)
    inward = (ahead + x * (back - ahead), gy)

    def member(step_y, flip):
        other_y = lax.rem(y + step_y, 4)
        other_x = 1 - x if flip else x
        return other_y, other_x, (base + 2 * other_y + other_x, gy)

    members = [member(s, f) for f in (False, True) for s in range(4) if f or s]

    def remote(src, dst, send, recv, to_device):
        return pltpu.make_async_remote_copy(
            src_ref=src, dst_ref=dst, send_sem=send, recv_sem=recv, device_id=to_device, device_id_type=MESH
        )

    barrier = pltpu.get_barrier_semaphore()
    greeted = [m[2] for m in members] + [outward, inward, on_chip, off_chip]
    for device in greeted:
        pl.semaphore_signal(barrier, inc=1, device_id=device, device_id_type=MESH)

    load_maps = pltpu.make_async_copy(leaf.at[0, :, pl.ds(0, 2 * E), :], lm, local_sem.at[0])
    load_maps.start()
    load_traces = pltpu.make_async_copy(traces.at[0], tv, local_sem.at[1])
    load_traces.start()
    mine = pl.ds(pl.multiple_of(x * 512, 512), 512)
    theirs = pl.ds(pl.multiple_of((1 - x) * 512, 512), 512)
    load_outer = pltpu.make_async_copy(traces.at[0, :, x, :, mine], to.at[x], local_sem.at[2])
    load_outer.start()

    load_maps.wait()
    eye = lax.broadcasted_iota(jnp.int32, (E, E), 0) == lax.broadcasted_iota(jnp.int32, (E, E), 1)
    lane_block = lax.div(lax.broadcasted_iota(jnp.int32, (1, E), 1), PB)
    face = pl.ds(pl.multiple_of((1 - x) * E, E), E)
    outer = pl.ds(pl.multiple_of(x * E, E), E)
    for j in range(2):
        for kind, edge, span in ((0, 1 - x, face), (2, x, outer)):
            ports = jnp.zeros((1, E), F32)
            for b in range(E // PB):
                ports = jnp.where(lane_block == b, decap_admittance * mask[0, j, edge, b].astype(F32), ports)
            m0[x, kind, j] = lm[j, span, span] + jnp.where(eye, ports, 0.0)
        m0[x, 1, j] = lm[j, face, outer]

    pl.semaphore_wait(barrier, len(greeted))
    sends = []

    def begin(copy):
        copy.start()
        sends.append(copy)
        return copy

    row_out = 1 - core
    row_off = core
    m0_copies = [begin(remote(m0.at[x, k], m0.at[x, k], m0_send.at[k], m0_recv.at[k], partner)) for k in range(3)]
    copy_tc = begin(remote(traces.at[0, row_out, 3 - core], tc, early_send.at[0], early_recv.at[0], on_chip))
    copy_tx = begin(remote(traces.at[0, row_off, 2 + core], tx, early_send.at[1], early_recv.at[1], off_chip))
    copy_out = begin(remote(traces.at[0, :, x, :, mine], te.at[1 - x], early_send.at[2], early_recv.at[2], outward))
    edge_off = pl.ds(pl.multiple_of((2 + core) * E, E), E)
    copy_rx = begin(
        remote(leaf.at[0, row_off, pl.ds(0, 2 * E), edge_off], rx, early_send.at[3], early_recv.at[3], partner)
    )

    def m0_other(k):
        return remote(m0.at[1 - x, k], m0.at[1 - x, k], m0_send.at[k], m0_recv.at[k], partner)

    for k in range(3):
        m0_other(k).wait_recv()
    copy_to = begin(remote(traces.at[0, :, x, :, theirs], to.at[x], early_send.at[4], early_recv.at[4], partner))

    systems = [m0[0, 0, j] + m0[1, 0, j] for j in range(2)]
    sides = [jnp.concatenate([m0[0, 1, j], m0[1, 1, j]], axis=1) for j in range(2)]
    solved = solve_all(systems, sides)
    for j in range(2):
        ww, ew, ee = merged(m0[0, 2, j], m0[1, 2, j], sides[j], solved[j])
        m1[y, j, 0] = ww
        m1[y, j, 1] = ew
        m1[y, j, 2] = ee
        xt0[j] = jnp.transpose(solved[j])
    for s in range(1, 4):
        begin(remote(m1.at[y], m1.at[y], m1_send.at[s], m1_recv.at[y], member(s, False)[2]))

    remote(to.at[1 - x], to.at[1 - x], early_send.at[4], early_recv.at[4], partner).wait_recv()
    begin(remote(to.at[1 - x], te.at[x], early_send.at[5], early_recv.at[5], inward))

    load_traces.wait()
    copy_rx.wait_recv()
    xf = x.astype(F32)

    def placed(block, right):
        return jnp.concatenate([block * (1.0 - right), block * right], axis=0)

    for row, off in ((row_out, False), (row_off, True)):
        inner = pl.ds(pl.multiple_of((3 - row) * E, E), E)
        rim = pl.ds(pl.multiple_of((2 + row) * E, E), E)
        xt = xt0[row]
        through = [m0[0, 0, row] + m0[1, 0, row], lm[row, face, inner], lm[row, face, rim]]
        direct = [
            jnp.transpose(jnp.concatenate([m0[0, 1, row], m0[1, 1, row]], axis=1)),
            placed(lm[row, outer, inner], xf),
            placed(lm[row, outer, rim], xf),
        ]
        if off:
            through.append(rx[outer, :])
            direct.append(placed(rx[face, :], 1.0 - xf))
        coefficient = 0.5 * (jnp.concatenate(direct, axis=1) - exact(xt, jnp.concatenate(through, axis=1)))
        high, low = halves(coefficient)
        width = coefficient.shape[1]
        q_hi[row, :, :width] = high
        q_lo[row, :, :width] = low

    copy_tc.wait_recv()
    copy_tx.wait_recv()

    def partial_load(start, slot):
        columns = pl.ds(pl.multiple_of(start, 256), 256)
        seam = tv[0, 3, :, columns] + tv[1, 2, :, columns]
        for row, off in ((row_out, False), (row_off, True)):
            rim = tv[row, 2 + row, :, columns]
            parts = [tv[row, 1 - x, :, columns], seam]
            parts += [rim, tx[:, columns]] if off else [rim + tc[:, columns]]
            data = jnp.concatenate(parts, axis=0)
            width = data.shape[0]
            load = split_dot((q_hi[row, :, :width], q_lo[row, :, :width]), halves(data))
            ps[slot, row] = load[:, :E]
            ps[slot + 1, row] = load[:, E:]

    for i in range(2):
        partial_load((1 - x) * 512 + i * 256, (1 - x) * 4 + 2 * i)
        for q in (2 * i, 2 * i + 1):
            begin(remote(ps.at[(1 - x) * 4 + q], pr.at[q], pr_send.at[q], pr_recv.at[q], partner))
    for i in range(2):
        partial_load(x * 512 + i * 256, x * 4 + 2 * i)

    for s in range(1, 4):
        other = member(s, False)
        remote(m1.at[y], m1.at[other[0]], m1_send.at[s], m1_recv.at[other[0]], other[2]).wait_recv()
    pairs = [(m, j) for m in range(2) for j in range(2)]
    systems = [m1[2 * m, j, 2] + m1[2 * m + 1, j, 0] for m, j in pairs]
    sides = [jnp.concatenate([m1[2 * m, j, 1], jnp.transpose(m1[2 * m + 1, j, 1])], axis=1) for m, j in pairs]
    solved = solve_all(systems, sides)
    for (m, j), side, s in zip(pairs, sides, solved):
        ww, ew, ee = merged(m1[2 * m, j, 0], m1[2 * m + 1, j, 2], side, s)
        m2[m, j, 0] = ww
        m2[m, j, 1] = ew
        m2[m, j, 2] = ee
        xt1[m, j] = jnp.transpose(s)

    load_outer.wait()
    remote(to.at[1 - x], te.at[1 - x], early_send.at[2], early_recv.at[2], inward).wait_recv()
    remote(to.at[1 - x], te.at[x], early_send.at[5], early_recv.at[5], outward).wait_recv()
    alphas = []
    for j in range(2):
        top = jnp.concatenate([m1[y, j, 0], jnp.transpose(m1[y, j, 1])], axis=1)
        bottom = jnp.concatenate([m1[y, j, 1], m1[y, j, 2]], axis=1)
        alphas.append(halves(0.5 * jnp.concatenate([top, bottom], axis=0)))
    for s in (1, 2, 3, 0):
        q, _, device = member(s, False)
        remote(ps.at[q], pr.at[q], pr_send.at[q], pr_recv.at[q], partner).wait_recv()
        columns = pl.ds(pl.multiple_of(q * E, E), E)
        for j in range(2):
            data = jnp.concatenate([to[e, j, :, columns] + te[e, j, :, columns] for e in range(2)], axis=0)
            load = ps[x * 4 + q, j] + pr[q, j] + split_dot(alphas[j], halves(data))
            if s:
                total[q, j] = load
            else:
                a2[y, j] = load
        if s:
            begin(remote(total.at[q], a2.at[y], a2_send.at[s], a2_recv.at[y], device))

    systems = [m2[0, j, 2] + m2[1, j, 0] for j in range(2)]
    sides = [jnp.concatenate([m2[0, j, 1], jnp.transpose(m2[1, j, 1])], axis=1) for j in range(2)]
    solved = solve_all(systems, sides)
    last = [jnp.transpose(s) for s in solved]

    for s in range(1, 4):
        other = member(s, False)
        remote(total.at[0], a2.at[other[0]], a2_send.at[s], a2_recv.at[other[0]], other[2]).wait_recv()
    for j in range(2):
        boxes = []
        for m in range(2):
            left, right = a2[2 * m, j], a2[2 * m + 1, j]
            ends = jnp.concatenate([left[:E], right[E:]], axis=0)
            boxes.append(ends - near(xt1[m, j], left[E:] + right[:E]))
        left, right = boxes
        ends = jnp.concatenate([left[:E], right[E:]], axis=0)
        fin[j] = ends - near(last[j], left[E:] + right[:E])
    own = pl.ds(pl.multiple_of((x * 4 + y) * E, E), E)
    for i, (_, _, device) in enumerate(members):
        begin(remote(fin, box_loads.at[0, :, :, own], fin_send.at[i], fin_recv.at[x * 4 + y], device))
    keep = pltpu.make_async_copy(fin, box_loads.at[0, :, :, own], local_sem.at[3])
    keep.start()

    for j in range(2):
        ww, ew, ee = merged(m2[0, j, 0], m2[1, j, 2], sides[j], solved[j])
        box_maps[0, j, :E, :E] = ww
        box_maps[0, j, E:, :E] = ew
        box_maps[0, j, :E, E:] = jnp.transpose(ew)
        box_maps[0, j, E:, E:] = ee

    for other_y, other_x, device in members:
        slot = other_x * 4 + other_y
        columns = pl.ds(pl.multiple_of(slot * E, E), E)
        remote(fin, box_loads.at[0, :, :, columns], fin_send.at[0], fin_recv.at[slot], device).wait_recv()
    keep.wait()
    for copy in sends:
        copy.wait_send()


def body(traces, leaf_maps, decap_mask):
    size_x, size_y = lax.axis_size("gx"), lax.axis_size("gy")
    dma = pltpu.SemaphoreType.DMA
    return pl.pallas_call(
        functools.partial(kernel, size_x, size_y),
        out_shape=(
            jax.ShapeDtypeStruct((1, 2, 2 * E, 2 * E), F32),
            jax.ShapeDtypeStruct((1, 2, 2 * E, K), F32),
        ),
        in_specs=[
            pl.BlockSpec(memory_space=pltpu.SMEM),
            pl.BlockSpec(memory_space=pl.ANY),
            pl.BlockSpec(memory_space=pl.ANY),
        ],
        out_specs=(pl.BlockSpec(memory_space=pltpu.VMEM), pl.BlockSpec(memory_space=pl.ANY)),
        scratch_shapes=[
            pltpu.VMEM((2, 2 * E, 4 * E), F32),
            pltpu.VMEM((2, 4, E, K), F32),
            pltpu.VMEM((2, 3, 2, E, E), F32),
            pltpu.VMEM((4, 2, 3, E, E), F32),
            pltpu.VMEM((2 * E, E), F32),
            pltpu.VMEM((2, 2, E, 512), F32),
            pltpu.VMEM((2, 2, E, 512), F32),
            pltpu.VMEM((E, K), F32),
            pltpu.VMEM((E, K), F32),
            pltpu.VMEM((2, 2 * E, E), F32),
            pltpu.VMEM((2, 2 * E, 4 * E), BF16),
            pltpu.VMEM((2, 2 * E, 4 * E), BF16),
            pltpu.VMEM((8, 2, 2 * E, E), F32),
            pltpu.VMEM((4, 2, 2 * E, E), F32),
            pltpu.VMEM((4, 2, 2 * E, E), F32),
            pltpu.VMEM((4, 2, 2 * E, E), F32),
            pltpu.VMEM((2, 2, 2 * E, E), F32),
            pltpu.VMEM((2, 2, 3, E, E), F32),
            pltpu.VMEM((2, 2 * E, E), F32),
            dma((4,)), dma((6,)), dma((6,)), dma((3,)), dma((3,)), dma((4,)), dma((4,)),
            dma((4,)), dma((4,)), dma((4,)), dma((4,)), dma((7,)), dma((8,)),
        ],
        compiler_params=pltpu.CompilerParams(
            collective_id=0, has_side_effects=True, vmem_limit_bytes=48 * 1024 * 1024
        ),
    )(decap_mask, traces, leaf_maps)


def solution(mesh):
    placed = (P("gx", "gy", None, None, None), P("gx", "gy", None, None), P("gx", "gy", None, None))
    return jax.shard_map(
        body,
        mesh=mesh,
        in_specs=placed,
        out_specs=(P("gx", "gy", None, None), P("gx", "gy", None, None)),
        check_vma=False,
    )
```

```python
import functools

import jax
import jax.numpy as jnp
from jax import lax
from jax.experimental import pallas as pl
from jax.experimental.pallas import tpu as pltpu
from jax.sharding import PartitionSpec as P

E = 128
K = 1024
PB = 16
F32 = jnp.float32
BF16 = jnp.bfloat16
NB = 32
STEP = 4
MESH = pl.DeviceIdType.MESH

decap_admittance = 2.0


def exact(left, right):
    return jnp.dot(left, right, precision=lax.Precision.HIGHEST, preferred_element_type=F32)


def halves(a):
    high = a.astype(BF16)
    return high, (a - high.astype(F32)).astype(BF16)


def split_dot(left, right):
    lh, ll = left
    rh, rl = right
    dot = functools.partial(jnp.dot, preferred_element_type=F32)
    return dot(lh, rl) + dot(ll, rh) + dot(lh, rh)


def near(left, right):
    return split_dot(halves(left), halves(right))


def invert_blocks(packed):
    shape = packed.shape
    lane = lax.broadcasted_iota(jnp.int32, shape, 1)
    row = lax.broadcasted_iota(jnp.int32, shape, 0)
    place = lax.rem(lane, NB)
    block = lane - place
    place8, block8 = place[:8], block[:8]
    steps = range(STEP)
    for k in range(0, NB, STEP):
        columns = [jnp.take_along_axis(packed, block + (k + j), axis=1) for j in steps]
        rows = [jnp.broadcast_to(packed[k + i : k + i + 1, :], (8, shape[1])) for i in steps]
        a = [[jnp.take_along_axis(rows[i], block8 + (k + j), axis=1) for j in steps] for i in steps]
        pivots8 = (place8 >= k) & (place8 < k + STEP)
        rows = [jnp.where(place8 == k + i, 1.0, jnp.where(pivots8, 0.0, rows[i])) for i in steps]
        for p in steps:
            inverse = 1.0 / a[p][p]
            factors = [a[i][p] for i in steps]
            for j in range(p + 1, STEP):
                a[p][j] = a[p][j] * inverse
            rows[p] = rows[p] * inverse
            for i in steps:
                if i != p:
                    for j in range(p + 1, STEP):
                        a[i][j] = a[i][j] - factors[i] * a[p][j]
                    rows[i] = rows[i] - factors[i] * rows[p]
        wide = [jnp.broadcast_to(r[:1], shape) for r in rows]
        new = jnp.where((place >= k) & (place < k + STEP), 0.0, packed)
        for j in steps:
            new = new - columns[j] * wide[j]
        for j in steps:
            new = jnp.where(row == k + j, wide[j], new)
        packed = new
    return packed


def solve_all(systems, sides):
    n = E
    blocks = [s[:NB, :NB] for s in systems]
    for p in range(0, n, NB):
        packed = invert_blocks(jnp.concatenate([blocks[i % len(blocks)] for i in range(E // NB)], axis=1))
        inverses = [packed[:, i * NB : (i + 1) * NB] for i in range(len(blocks))]
        if callable(sides):
            sides = sides()
        last = p + NB == n
        if not last:
            ahead = slice(p + NB, p + 2 * NB)
            blocks = [
                s[ahead, ahead] - exact(s[ahead, p : p + NB], exact(inverse, s[p : p + NB, ahead]))
                for s, inverse in zip(systems, inverses)
            ]
        next_systems, next_sides = [], []
        for s, r, inverse in zip(systems, sides, inverses):
            full = r if last else jnp.concatenate([s[:, p + NB :], r], axis=1)
            pivot = exact(inverse, full[p : p + NB])
            parts = []
            if p:
                parts.append(full[:p] - exact(s[:p, p : p + NB], pivot))
            parts.append(pivot)
            if not last:
                parts.append(full[p + NB :] - exact(s[p + NB :, p : p + NB], pivot))
            full = jnp.concatenate(parts, axis=0)
            if not last:
                rest = n - p - NB
                next_systems.append(jnp.concatenate([jnp.zeros((n, p + NB), F32), full[:, :rest]], axis=1))
                full = full[:, rest:]
            next_sides.append(full)
        systems, sides = next_systems, next_sides
    return sides


def merged(outer_left, outer_right, side, solved):
    across = jnp.transpose(side)
    ww = outer_left - exact(across[:E], solved[:, :E])
    low = exact(across[E:], solved)
    return ww, -low[:, :E], outer_right - low[:, E:]


def kernel(
    size_x, size_y,
    mask, traces, leaf, box_maps, box_loads,
    lm, tv, m0, m1, rx, to, te, tc, tx, xt0, ends, q_hi, q_lo, ps, pr, total, a2, xt1, m2, fin, got,
    local_sem, early_send, early_recv, m0_send, m0_recv, m1_send, m1_recv,
    pr_send, pr_recv, a2_send, a2_recv, fin_send, fin_recv, keep_sem,
):
    gx = lax.axis_index("gx")
    gy = lax.axis_index("gy")
    x = lax.rem(gx, 2)
    y = lax.rem(lax.div(gx, 2), 4)
    base = gx - lax.rem(gx, 8)
    core = lax.rem(gy, 2)
    partner = (gx + 1 - 2 * x, gy)
    back = lax.rem(gx + size_x - 2, size_x)
    ahead = lax.rem(gx + 2, size_x)
    on_chip = (gx, gy + 1 - 2 * core)
    off_chip = (gx + 1 - 2 * x, lax.rem(gy + size_y + 2 * core - 1, size_y))
    outward = (back + x * (ahead - back), gy)
    inward = (ahead + x * (back - ahead), gy)

    def member(step_y, flip):
        other_y = lax.rem(y + step_y, 4)
        other_x = 1 - x if flip else x
        return other_y, other_x, (base + 2 * other_y + other_x, gy)

    members = [member(s, f) for f in (False, True) for s in range(4) if f or s]

    def remote(src, dst, send, recv, to_device):
        return pltpu.make_async_remote_copy(
            src_ref=src, dst_ref=dst, send_sem=send, recv_sem=recv, device_id=to_device, device_id_type=MESH
        )

    barrier = pltpu.get_barrier_semaphore()
    greeted = [m[2] for m in members] + [outward, inward, on_chip, off_chip]
    for device in greeted:
        pl.semaphore_signal(barrier, inc=1, device_id=device, device_id_type=MESH)

    load_maps = pltpu.make_async_copy(leaf.at[0, :, pl.ds(0, 2 * E), :], lm, local_sem.at[0])
    load_maps.start()
    load_traces = pltpu.make_async_copy(traces.at[0], tv, local_sem.at[1])
    load_traces.start()

    load_maps.wait()
    eye = lax.broadcasted_iota(jnp.int32, (E, E), 0) == lax.broadcasted_iota(jnp.int32, (E, E), 1)
    lane_block = lax.div(lax.broadcasted_iota(jnp.int32, (1, E), 1), PB)
    face = pl.ds(pl.multiple_of((1 - x) * E, E), E)
    outer = pl.ds(pl.multiple_of(x * E, E), E)
    for j in range(2):
        for kind, edge, span in ((0, 1 - x, face), (2, x, outer)):
            ports = jnp.zeros((1, E), F32)
            for b in range(E // PB):
                ports = jnp.where(lane_block == b, decap_admittance * mask[0, j, edge, b].astype(F32), ports)
            m0[x, kind, j] = lm[j, span, span] + jnp.where(eye, ports, 0.0)
        m0[x, 1, j] = lm[j, face, outer]

    pl.semaphore_wait(barrier, len(greeted))
    sends = []

    def begin(copy):
        copy.start()
        sends.append(copy)
        return copy

    row_out = 1 - core
    row_off = core
    m0_copies = [begin(remote(m0.at[x, k], m0.at[x, k], m0_send.at[k], m0_recv.at[k], partner)) for k in range(3)]
    copy_tc = begin(remote(traces.at[0, row_out, 3 - core], tc, early_send.at[0], early_recv.at[0], on_chip))
    copy_tx = begin(remote(traces.at[0, row_off, 2 + core], tx, early_send.at[1], early_recv.at[1], off_chip))
    mine = pl.ds(pl.multiple_of(x * 512, 512), 512)
    theirs = pl.ds(pl.multiple_of((1 - x) * 512, 512), 512)
    load_outer = pltpu.make_async_copy(traces.at[0, :, x, :, mine], to.at[x], local_sem.at[2])
    load_outer.start()
    begin(remote(traces.at[0, :, x, :, mine], te.at[1 - x], early_send.at[3], early_recv.at[3], outward))
    edge_off = pl.ds(pl.multiple_of((2 + core) * E, E), E)

    def m0_other(k):
        return remote(m0.at[1 - x, k], m0.at[1 - x, k], m0_send.at[k], m0_recv.at[k], partner)

    m0_other(0).wait_recv()
    copy_rx = begin(
        remote(leaf.at[0, row_off, pl.ds(0, 2 * E), edge_off], rx, early_send.at[2], early_recv.at[2], partner)
    )

    systems = [m0[0, 0, j] + m0[1, 0, j] for j in range(2)]

    def pair_sides():
        m0_other(1).wait_recv()
        begin(remote(traces.at[0, :, x, :, theirs], to.at[x], early_send.at[4], early_recv.at[4], partner))
        return [jnp.concatenate([m0[0, 1, j], m0[1, 1, j]], axis=1) for j in range(2)]

    solved = solve_all(systems, pair_sides)
    sides = [jnp.concatenate([m0[0, 1, j], m0[1, 1, j]], axis=1) for j in range(2)]
    m0_other(2).wait_recv()
    for j in range(2):
        ww, ew, ee = merged(m0[0, 2, j], m0[1, 2, j], sides[j], solved[j])
        m1[y, 0, j] = ww
        m1[y, 1, j] = ew
        m1[y, 2, j] = ee
        xt0[j] = jnp.transpose(solved[j])
        ends[j, :E] = 0.5 * jnp.concatenate([ww, jnp.transpose(ew)], axis=1)
        ends[j, E:] = 0.5 * jnp.concatenate([ew, ee], axis=1)

    def m1_copy(s, order, owner, device):
        first = 2 * (1 - lax.rem(owner, 2))
        kind = (first, 1, 2 - first)[order]
        return remote(
            m1.at[owner, kind], m1.at[owner, kind], m1_send.at[order, s], m1_recv.at[order, owner], device
        )

    for order in range(3):
        for s in (1, 3, 2):
            begin(m1_copy(s, order, y, member(s, False)[2]))

    remote(to.at[1 - x], to.at[1 - x], early_send.at[4], early_recv.at[4], partner).wait_recv()
    begin(remote(to.at[1 - x], te.at[x], early_send.at[5], early_recv.at[5], inward))

    load_traces.wait()
    copy_rx.wait_recv()
    xf = x.astype(F32)

    def placed(block, right):
        return jnp.concatenate([block * (1.0 - right), block * right], axis=0)

    for row, off in ((row_out, False), (row_off, True)):
        inner = pl.ds(pl.multiple_of((3 - row) * E, E), E)
        rim = pl.ds(pl.multiple_of((2 + row) * E, E), E)
        xt = xt0[row]
        through = [m0[0, 0, row] + m0[1, 0, row], lm[row, face, inner], lm[row, face, rim]]
        direct = [
            jnp.transpose(jnp.concatenate([m0[0, 1, row], m0[1, 1, row]], axis=1)),
            placed(lm[row, outer, inner], xf),
            placed(lm[row, outer, rim], xf),
        ]
        if off:
            through.append(rx[outer, :])
            direct.append(placed(rx[face, :], 1.0 - xf))
        coefficient = 0.5 * (jnp.concatenate(direct, axis=1) - exact(xt, jnp.concatenate(through, axis=1)))
        high, low = halves(coefficient)
        width = coefficient.shape[1]
        q_hi[row, :, :width] = high
        q_lo[row, :, :width] = low

    copy_tc.wait_recv()
    copy_tx.wait_recv()

    def partial_load(i):
        half = lax.rem(1 - x + i // 2, 2)
        slot = half * 4 + 2 * (i % 2)
        columns = pl.ds(pl.multiple_of(half * 512 + (i % 2) * 256, 256), 256)
        seam = tv[0, 3, :, columns] + tv[1, 2, :, columns]
        for row, off in ((row_out, False), (row_off, True)):
            rim = tv[row, 2 + row, :, columns]
            parts = [tv[row, 1 - x, :, columns], seam]
            parts += [rim, tx[:, columns]] if off else [rim + tc[:, columns]]
            data = jnp.concatenate(parts, axis=0)
            width = data.shape[0]
            load = split_dot((q_hi[row, :, :width], q_lo[row, :, :width]), halves(data))
            ps[slot, row] = load[:, :E]
            ps[slot + 1, row] = load[:, E:]

    for i in range(2):
        partial_load(i)
        for q in (2 * i, 2 * i + 1):
            begin(remote(ps.at[(1 - x) * 4 + q], pr.at[q], pr_send.at[q], pr_recv.at[q], partner))
    for i in range(2):
        partial_load(2 + i)

    for s in range(1, 4):
        other = member(s, False)
        for order in range(2):
            m1_copy(s, order, other[0], other[2]).wait_recv()
    pairs = [(m, j) for m in range(2) for j in range(2)]
    systems = [m1[2 * m, 2, j] + m1[2 * m + 1, 0, j] for m, j in pairs]
    sides = [jnp.concatenate([m1[2 * m, 1, j], jnp.transpose(m1[2 * m + 1, 1, j])], axis=1) for m, j in pairs]
    solved = solve_all(systems, sides)
    for s in range(1, 4):
        other = member(s, False)
        m1_copy(s, 2, other[0], other[2]).wait_recv()
    for (m, j), side, s in zip(pairs, sides, solved):
        ww, ew, ee = merged(m1[2 * m, 0, j], m1[2 * m + 1, 2, j], side, s)
        m2[m, j, 0] = ww
        m2[m, j, 1] = ew
        m2[m, j, 2] = ee
        xt1[m, j] = jnp.transpose(s)

    load_outer.wait()
    remote(to.at[1 - x], te.at[1 - x], early_send.at[3], early_recv.at[3], inward).wait_recv()
    remote(to.at[1 - x], te.at[x], early_send.at[5], early_recv.at[5], outward).wait_recv()
    alphas = [halves(ends[j]) for j in range(2)]

    def share(q):
        device = (base + 2 * q + x, gy)
        return remote(total.at[q], a2.at[y], a2_send.at[q], a2_recv.at[y], device)

    def pair_load(q):
        remote(ps.at[q], pr.at[q], pr_send.at[q], pr_recv.at[q], partner).wait_recv()
        for j in range(2):
            columns = slice(q * E, (q + 1) * E)
            data = jnp.concatenate([to[e, j, :, columns] + te[e, j, :, columns] for e in range(2)], axis=0)
            total[q, j] = ps[x * 4 + q, j] + pr[q, j] + split_dot(alphas[j], halves(data))

        @pl.when(y != q)
        def _():
            share(q).start()

        @pl.when(y == q)
        def _():
            a2[q] = total[q]

    for q in range(4):
        pair_load(q)

    systems = [m2[0, j, 2] + m2[1, j, 0] for j in range(2)]
    sides = [jnp.concatenate([m2[0, j, 1], jnp.transpose(m2[1, j, 1])], axis=1) for j in range(2)]
    solved = solve_all(systems, sides)
    last = [jnp.transpose(s) for s in solved]

    for s in range(1, 4):
        other = member(s, False)
        remote(total.at[0], a2.at[other[0]], a2_send.at[s], a2_recv.at[other[0]], other[2]).wait_recv()
    own_slot = x * 4 + y
    others = [member(s, False) for s in (1, 3, 2)]

    def gather(n, src, row, slot, device):
        dst = got.at[row, slot]
        return remote(dst if src is None else src, dst, fin_send.at[n], fin_recv.at[row, slot], device)

    keeps = []

    def keep(src, row, slot):
        columns = pl.ds(pl.multiple_of(slot * E, E), E)
        copy = pltpu.make_async_copy(src, box_loads.at[0, row, :, columns], keep_sem.at[row, slot])
        copy.start()
        keeps.append(copy)

    def arrive(n, row, slot, device):
        gather(n, fin.at[row], row, slot, device).wait_recv()
        keep(got.at[row, slot], row, slot)

    for j in (0, 1):
        boxes = []
        for m in range(2):
            left, right = a2[2 * m, j], a2[2 * m + 1, j]
            kept = jnp.concatenate([left[:E], right[E:]], axis=0)
            boxes.append(kept - near(xt1[m, j], left[E:] + right[:E]))
        left, right = boxes
        kept = jnp.concatenate([left[:E], right[E:]], axis=0)
        fin[j] = kept - near(last[j], left[E:] + right[:E])
        begin(gather(7 * j, fin.at[j], j, own_slot, partner))
        for i, (_, _, device) in enumerate(others):
            begin(gather(7 * j + 1 + i, fin.at[j], j, own_slot, device))
        keep(fin.at[j], j, own_slot)

    partner_slot = (1 - x) * 4 + y
    def pass_on(i):
        slot = x * 4 + others[i][0]
        arrive(1 + i, 0, slot, others[i][2])
        begin(gather(4 + i, None, 0, slot, partner))

    pass_on(0)
    pass_on(1)
    arrive(7, 1, partner_slot, partner)
    for i, (_, _, device) in enumerate(others):
        begin(gather(11 + i, None, 1, partner_slot, device))
    pass_on(2)

    for j in range(2):
        ww, ew, ee = merged(m2[0, j, 0], m2[1, j, 2], sides[j], solved[j])
        box_maps[0, j, :E, :E] = ww
        box_maps[0, j, E:, :E] = ew
        box_maps[0, j, :E, E:] = jnp.transpose(ew)
        box_maps[0, j, E:, E:] = ee

    for i, (other_y, _, device) in enumerate(others):
        arrive(8 + i, 1, x * 4 + other_y, device)
        arrive(11 + i, 1, (1 - x) * 4 + other_y, device)
    arrive(0, 0, partner_slot, partner)
    for i, (other_y, _, _) in enumerate(others):
        arrive(4 + i, 0, (1 - x) * 4 + other_y, partner)
    for copy in keeps:
        copy.wait()
    for copy in sends:
        copy.wait_send()
    for q in range(4):
        @pl.when(y != q)
        def _(q=q):
            share(q).wait_send()


def body(traces, leaf_maps, decap_mask):
    size_x, size_y = lax.axis_size("gx"), lax.axis_size("gy")
    dma = pltpu.SemaphoreType.DMA
    return pl.pallas_call(
        functools.partial(kernel, size_x, size_y),
        out_shape=(
            jax.ShapeDtypeStruct((1, 2, 2 * E, 2 * E), F32),
            jax.ShapeDtypeStruct((1, 2, 2 * E, K), F32),
        ),
        in_specs=[
            pl.BlockSpec(memory_space=pltpu.SMEM),
            pl.BlockSpec(memory_space=pl.ANY),
            pl.BlockSpec(memory_space=pl.ANY),
        ],
        out_specs=(pl.BlockSpec(memory_space=pltpu.VMEM), pl.BlockSpec(memory_space=pl.ANY)),
        scratch_shapes=[
            pltpu.VMEM((2, 2 * E, 4 * E), F32),
            pltpu.VMEM((2, 4, E, K), F32),
            pltpu.VMEM((2, 3, 2, E, E), F32),
            pltpu.VMEM((4, 3, 2, E, E), F32),
            pltpu.VMEM((2 * E, E), F32),
            pltpu.VMEM((2, 2, E, 512), F32),
            pltpu.VMEM((2, 2, E, 512), F32),
            pltpu.VMEM((E, K), F32),
            pltpu.VMEM((E, K), F32),
            pltpu.VMEM((2, 2 * E, E), F32),
            pltpu.VMEM((2, 2 * E, 2 * E), F32),
            pltpu.VMEM((2, 2 * E, 4 * E), BF16),
            pltpu.VMEM((2, 2 * E, 4 * E), BF16),
            pltpu.VMEM((8, 2, 2 * E, E), F32),
            pltpu.VMEM((4, 2, 2 * E, E), F32),
            pltpu.VMEM((4, 2, 2 * E, E), F32),
            pltpu.VMEM((4, 2, 2 * E, E), F32),
            pltpu.VMEM((2, 2, 2 * E, E), F32),
            pltpu.VMEM((2, 2, 3, E, E), F32),
            pltpu.VMEM((2, 2 * E, E), F32),
            pltpu.VMEM((2, 8, 2 * E, E), F32),
            dma((3,)), dma((6,)), dma((6,)), dma((3,)), dma((3,)), dma((3, 4)), dma((3, 4)),
            dma((4,)), dma((4,)), dma((4,)), dma((4,)), dma((14,)), dma((2, 8)), dma((2, 8)),
        ],
        compiler_params=pltpu.CompilerParams(
            collective_id=0, has_side_effects=True, vmem_limit_bytes=60 * 1024 * 1024
        ),
    )(decap_mask, traces, leaf_maps)


def solution(mesh):
    placed = (P("gx", "gy", None, None, None), P("gx", "gy", None, None), P("gx", "gy", None, None))
    return jax.shard_map(
        body,
        mesh=mesh,
        in_specs=placed,
        out_specs=(P("gx", "gy", None, None), P("gx", "gy", None, None)),
        check_vma=False,
    )
```

```python
import functools

import jax
import jax.numpy as jnp
from jax import lax
from jax.experimental import pallas as pl
from jax.experimental.pallas import tpu as pltpu
from jax.sharding import PartitionSpec as P

E = 128
K = 1024
PB = 16
F32 = jnp.float32
BF16 = jnp.bfloat16
NB = 32
STEP = 4
MESH = pl.DeviceIdType.MESH

decap_admittance = 2.0


def exact(left, right):
    return jnp.dot(left, right, precision=lax.Precision.HIGHEST, preferred_element_type=F32)


def halves(a):
    high = a.astype(BF16)
    return high, (a - high.astype(F32)).astype(BF16)


def split_dot(left, right):
    lh, ll = left
    rh, rl = right
    dot = functools.partial(jnp.dot, preferred_element_type=F32)
    return dot(lh, rl) + dot(ll, rh) + dot(lh, rh)


def near(left, right):
    return split_dot(halves(left), halves(right))


def invert_blocks(packed):
    shape = packed.shape
    lane = lax.broadcasted_iota(jnp.int32, shape, 1)
    row = lax.broadcasted_iota(jnp.int32, shape, 0)
    place = lax.rem(lane, NB)
    block = lane - place
    place8, block8 = place[:8], block[:8]
    steps = range(STEP)
    for k in range(0, NB, STEP):
        columns = [jnp.take_along_axis(packed, block + (k + j), axis=1) for j in steps]
        rows = [jnp.broadcast_to(packed[k + i : k + i + 1, :], (8, shape[1])) for i in steps]
        a = [[jnp.take_along_axis(rows[i], block8 + (k + j), axis=1) for j in steps] for i in steps]
        pivots8 = (place8 >= k) & (place8 < k + STEP)
        rows = [jnp.where(place8 == k + i, 1.0, jnp.where(pivots8, 0.0, rows[i])) for i in steps]
        for p in steps:
            inverse = 1.0 / a[p][p]
            factors = [a[i][p] for i in steps]
            for j in range(p + 1, STEP):
                a[p][j] = a[p][j] * inverse
            rows[p] = rows[p] * inverse
            for i in steps:
                if i != p:
                    for j in range(p + 1, STEP):
                        a[i][j] = a[i][j] - factors[i] * a[p][j]
                    rows[i] = rows[i] - factors[i] * rows[p]
        wide = [jnp.broadcast_to(r[:1], shape) for r in rows]
        new = jnp.where((place >= k) & (place < k + STEP), 0.0, packed)
        for j in steps:
            new = new - columns[j] * wide[j]
        for j in steps:
            new = jnp.where(row == k + j, wide[j], new)
        packed = new
    return packed


def solve_all(systems, sides):
    n = E
    blocks = [s[:NB, :NB] for s in systems]
    for p in range(0, n, NB):
        packed = invert_blocks(jnp.concatenate([blocks[i % len(blocks)] for i in range(E // NB)], axis=1))
        inverses = [packed[:, i * NB : (i + 1) * NB] for i in range(len(blocks))]
        if callable(sides):
            sides = sides()
        last = p + NB == n
        if not last:
            ahead = slice(p + NB, p + 2 * NB)
            blocks = [
                s[ahead, ahead] - exact(s[ahead, p : p + NB], exact(inverse, s[p : p + NB, ahead]))
                for s, inverse in zip(systems, inverses)
            ]
        next_systems, next_sides = [], []
        for s, r, inverse in zip(systems, sides, inverses):
            full = r if last else jnp.concatenate([s[:, p + NB :], r], axis=1)
            pivot = exact(inverse, full[p : p + NB])
            parts = []
            if p:
                parts.append(full[:p] - exact(s[:p, p : p + NB], pivot))
            parts.append(pivot)
            if not last:
                parts.append(full[p + NB :] - exact(s[p + NB :, p : p + NB], pivot))
            full = jnp.concatenate(parts, axis=0)
            if not last:
                rest = n - p - NB
                next_systems.append(jnp.concatenate([jnp.zeros((n, p + NB), F32), full[:, :rest]], axis=1))
                full = full[:, rest:]
            next_sides.append(full)
        systems, sides = next_systems, next_sides
    return sides


def merged(outer_left, outer_right, side, solved):
    across = jnp.transpose(side)
    ww = outer_left - near(across[:E], solved[:, :E])
    low = near(across[E:], solved)
    return ww, -low[:, :E], outer_right - low[:, E:]


def kernel(
    size_x, size_y,
    mask, traces, leaf, box_maps, box_loads,
    lm, tv, m0, m1, rx, to, te, tc, tx, xt0, ends, q_hi, q_lo, ps, pr, total, a2, xt1, m2, fin, got,
    local_sem, early_send, early_recv, m0_send, m0_recv, m1_send, m1_recv,
    pr_send, pr_recv, a2_send, a2_recv, fin_send, fin_recv, keep_sem,
):
    gx = lax.axis_index("gx")
    gy = lax.axis_index("gy")
    x = lax.rem(gx, 2)
    y = lax.rem(lax.div(gx, 2), 4)
    base = gx - lax.rem(gx, 8)
    core = lax.rem(gy, 2)
    partner = (gx + 1 - 2 * x, gy)
    back = lax.rem(gx + size_x - 2, size_x)
    ahead = lax.rem(gx + 2, size_x)
    on_chip = (gx, gy + 1 - 2 * core)
    off_chip = (gx + 1 - 2 * x, lax.rem(gy + size_y + 2 * core - 1, size_y))
    outward = (back + x * (ahead - back), gy)
    inward = (ahead + x * (back - ahead), gy)

    def member(step_y, flip):
        other_y = lax.rem(y + step_y, 4)
        other_x = 1 - x if flip else x
        return other_y, other_x, (base + 2 * other_y + other_x, gy)

    members = [member(s, f) for f in (False, True) for s in range(4) if f or s]

    def remote(src, dst, send, recv, to_device):
        return pltpu.make_async_remote_copy(
            src_ref=src, dst_ref=dst, send_sem=send, recv_sem=recv, device_id=to_device, device_id_type=MESH
        )

    barrier = pltpu.get_barrier_semaphore()
    greeted = [m[2] for m in members] + [outward, inward, on_chip, off_chip]
    for device in greeted:
        pl.semaphore_signal(barrier, inc=1, device_id=device, device_id_type=MESH)

    load_maps = pltpu.make_async_copy(leaf.at[0, :, pl.ds(0, 2 * E), :], lm, local_sem.at[0])
    load_maps.start()
    load_traces = pltpu.make_async_copy(traces.at[0], tv, local_sem.at[1])
    load_traces.start()

    load_maps.wait()
    eye = lax.broadcasted_iota(jnp.int32, (E, E), 0) == lax.broadcasted_iota(jnp.int32, (E, E), 1)
    lane_block = lax.div(lax.broadcasted_iota(jnp.int32, (1, E), 1), PB)
    face = pl.ds(pl.multiple_of((1 - x) * E, E), E)
    outer = pl.ds(pl.multiple_of(x * E, E), E)
    for j in range(2):
        for kind, edge, span in ((0, 1 - x, face), (2, x, outer)):
            ports = jnp.zeros((1, E), F32)
            for b in range(E // PB):
                ports = jnp.where(lane_block == b, decap_admittance * mask[0, j, edge, b].astype(F32), ports)
            m0[x, kind, j] = lm[j, span, span] + jnp.where(eye, ports, 0.0)
        m0[x, 1, j] = lm[j, face, outer]

    pl.semaphore_wait(barrier, len(greeted))
    sends = []

    def begin(copy):
        copy.start()
        sends.append(copy)
        return copy

    row_out = 1 - core
    row_off = core
    m0_copies = [begin(remote(m0.at[x, k], m0.at[x, k], m0_send.at[k], m0_recv.at[k], partner)) for k in range(3)]
    copy_tc = begin(remote(traces.at[0, row_out, 3 - core], tc, early_send.at[0], early_recv.at[0], on_chip))
    copy_tx = begin(remote(traces.at[0, row_off, 2 + core], tx, early_send.at[1], early_recv.at[1], off_chip))
    mine = pl.ds(pl.multiple_of(x * 512, 512), 512)
    theirs = pl.ds(pl.multiple_of((1 - x) * 512, 512), 512)
    load_outer = pltpu.make_async_copy(traces.at[0, :, x, :, mine], to.at[x], local_sem.at[2])
    load_outer.start()
    begin(remote(traces.at[0, :, x, :, mine], te.at[1 - x], early_send.at[3], early_recv.at[3], outward))
    edge_off = pl.ds(pl.multiple_of((2 + core) * E, E), E)

    def m0_other(k):
        return remote(m0.at[1 - x, k], m0.at[1 - x, k], m0_send.at[k], m0_recv.at[k], partner)

    m0_other(0).wait_recv()
    copy_rx = begin(
        remote(leaf.at[0, row_off, pl.ds(0, 2 * E), edge_off], rx, early_send.at[2], early_recv.at[2], partner)
    )

    systems = [m0[0, 0, j] + m0[1, 0, j] for j in range(2)]

    def pair_sides():
        m0_other(1).wait_recv()
        begin(remote(traces.at[0, :, x, :, theirs], to.at[x], early_send.at[4], early_recv.at[4], partner))
        return [jnp.concatenate([m0[0, 1, j], m0[1, 1, j]], axis=1) for j in range(2)]

    solved = solve_all(systems, pair_sides)
    sides = [jnp.concatenate([m0[0, 1, j], m0[1, 1, j]], axis=1) for j in range(2)]
    m0_other(2).wait_recv()
    for j in range(2):
        ww, ew, ee = merged(m0[0, 2, j], m0[1, 2, j], sides[j], solved[j])
        m1[y, 0, j] = ww
        m1[y, 1, j] = ew
        m1[y, 2, j] = ee
        xt0[j] = jnp.transpose(solved[j])
        ends[j, :E] = 0.5 * jnp.concatenate([ww, jnp.transpose(ew)], axis=1)
        ends[j, E:] = 0.5 * jnp.concatenate([ew, ee], axis=1)

    def m1_copy(s, order, owner, device):
        first = 2 * (1 - lax.rem(owner, 2))
        kind = (first, 1, 2 - first)[order]
        return remote(
            m1.at[owner, kind], m1.at[owner, kind], m1_send.at[order, s], m1_recv.at[order, owner], device
        )

    for order in range(3):
        for s in (1, 3, 2):
            begin(m1_copy(s, order, y, member(s, False)[2]))

    load_traces.wait()
    copy_rx.wait_recv()
    xf = x.astype(F32)

    def placed(block, right):
        return jnp.concatenate([block * (1.0 - right), block * right], axis=0)

    for row, off in ((row_out, False), (row_off, True)):
        inner = pl.ds(pl.multiple_of((3 - row) * E, E), E)
        rim = pl.ds(pl.multiple_of((2 + row) * E, E), E)
        xt = xt0[row]
        through = [m0[0, 0, row] + m0[1, 0, row], lm[row, face, inner], lm[row, face, rim]]
        direct = [
            jnp.transpose(jnp.concatenate([m0[0, 1, row], m0[1, 1, row]], axis=1)),
            placed(lm[row, outer, inner], xf),
            placed(lm[row, outer, rim], xf),
        ]
        if off:
            through.append(rx[outer, :])
            direct.append(placed(rx[face, :], 1.0 - xf))
        coefficient = 0.5 * (jnp.concatenate(direct, axis=1) - near(xt, jnp.concatenate(through, axis=1)))
        high, low = halves(coefficient)
        width = coefficient.shape[1]
        q_hi[row, :, :width] = high
        q_lo[row, :, :width] = low

    copy_tc.wait_recv()
    copy_tx.wait_recv()

    def partial_load(i):
        half = lax.rem(1 - x + i // 2, 2)
        slot = half * 4 + 2 * (i % 2)
        columns = pl.ds(pl.multiple_of(half * 512 + (i % 2) * 256, 256), 256)
        seam = tv[0, 3, :, columns] + tv[1, 2, :, columns]
        for row, off in ((row_out, False), (row_off, True)):
            rim = tv[row, 2 + row, :, columns]
            parts = [tv[row, 1 - x, :, columns], seam]
            parts += [rim, tx[:, columns]] if off else [rim + tc[:, columns]]
            data = jnp.concatenate(parts, axis=0)
            width = data.shape[0]
            load = split_dot((q_hi[row, :, :width], q_lo[row, :, :width]), halves(data))
            ps[slot, row] = load[:, :E]
            ps[slot + 1, row] = load[:, E:]

    for i in range(2):
        partial_load(i)
        for q in (2 * i, 2 * i + 1):
            begin(remote(ps.at[(1 - x) * 4 + q], pr.at[q], pr_send.at[q], pr_recv.at[q], partner))
    remote(to.at[1 - x], to.at[1 - x], early_send.at[4], early_recv.at[4], partner).wait_recv()
    begin(remote(to.at[1 - x], te.at[x], early_send.at[5], early_recv.at[5], inward))
    for i in range(2):
        partial_load(2 + i)

    for s in range(1, 4):
        other = member(s, False)
        for order in range(2):
            m1_copy(s, order, other[0], other[2]).wait_recv()
    pairs = [(m, j) for m in range(2) for j in range(2)]
    systems = [m1[2 * m, 2, j] + m1[2 * m + 1, 0, j] for m, j in pairs]
    sides = [jnp.concatenate([m1[2 * m, 1, j], jnp.transpose(m1[2 * m + 1, 1, j])], axis=1) for m, j in pairs]
    solved = solve_all(systems, sides)
    for s in range(1, 4):
        other = member(s, False)
        m1_copy(s, 2, other[0], other[2]).wait_recv()
    for (m, j), side, s in zip(pairs, sides, solved):
        ww, ew, ee = merged(m1[2 * m, 0, j], m1[2 * m + 1, 2, j], side, s)
        m2[m, j, 0] = ww
        m2[m, j, 1] = ew
        m2[m, j, 2] = ee
        xt1[m, j] = jnp.transpose(s)

    load_outer.wait()
    remote(to.at[1 - x], te.at[1 - x], early_send.at[3], early_recv.at[3], inward).wait_recv()
    remote(to.at[1 - x], te.at[x], early_send.at[5], early_recv.at[5], outward).wait_recv()
    alphas = [halves(ends[j]) for j in range(2)]

    def share(q):
        device = (base + 2 * q + x, gy)
        return remote(total.at[q], a2.at[y], a2_send.at[q], a2_recv.at[y], device)

    def pair_load(q):
        remote(ps.at[q], pr.at[q], pr_send.at[q], pr_recv.at[q], partner).wait_recv()
        for j in range(2):
            columns = slice(q * E, (q + 1) * E)
            data = jnp.concatenate([to[e, j, :, columns] + te[e, j, :, columns] for e in range(2)], axis=0)
            total[q, j] = ps[x * 4 + q, j] + pr[q, j] + split_dot(alphas[j], halves(data))

        @pl.when(y != q)
        def _():
            share(q).start()

        @pl.when(y == q)
        def _():
            a2[q] = total[q]

    for q in range(4):
        pair_load(q)

    systems = [m2[0, j, 2] + m2[1, j, 0] for j in range(2)]
    sides = [jnp.concatenate([m2[0, j, 1], jnp.transpose(m2[1, j, 1])], axis=1) for j in range(2)]
    solved = solve_all(systems, sides)
    last = [jnp.transpose(s) for s in solved]

    for s in range(1, 4):
        other = member(s, False)
        remote(total.at[0], a2.at[other[0]], a2_send.at[s], a2_recv.at[other[0]], other[2]).wait_recv()
    own_slot = x * 4 + y
    others = [member(s, False) for s in (1, 3, 2)]

    def gather(n, src, row, slot, device):
        dst = got.at[row, slot]
        return remote(dst if src is None else src, dst, fin_send.at[n], fin_recv.at[row, slot], device)

    keeps = []

    def keep(src, row, slot):
        columns = pl.ds(pl.multiple_of(slot * E, E), E)
        copy = pltpu.make_async_copy(src, box_loads.at[0, row, :, columns], keep_sem.at[row, slot])
        copy.start()
        keeps.append(copy)

    def arrive(n, row, slot, device):
        gather(n, fin.at[row], row, slot, device).wait_recv()
        keep(got.at[row, slot], row, slot)

    for j in (0, 1):
        boxes = []
        for m in range(2):
            left, right = a2[2 * m, j], a2[2 * m + 1, j]
            kept = jnp.concatenate([left[:E], right[E:]], axis=0)
            boxes.append(kept - near(xt1[m, j], left[E:] + right[:E]))
        left, right = boxes
        kept = jnp.concatenate([left[:E], right[E:]], axis=0)
        fin[j] = kept - near(last[j], left[E:] + right[:E])
        begin(gather(7 * j, fin.at[j], j, own_slot, partner))
        for i, (_, _, device) in enumerate(others):
            begin(gather(7 * j + 1 + i, fin.at[j], j, own_slot, device))
        keep(fin.at[j], j, own_slot)

    partner_slot = (1 - x) * 4 + y
    def pass_on(i):
        slot = x * 4 + others[i][0]
        arrive(1 + i, 0, slot, others[i][2])
        begin(gather(4 + i, None, 0, slot, partner))

    pass_on(0)
    pass_on(1)
    arrive(7, 1, partner_slot, partner)
    for i, (_, _, device) in enumerate(others):
        begin(gather(11 + i, None, 1, partner_slot, device))
    pass_on(2)

    for j in range(2):
        ww, ew, ee = merged(m2[0, j, 0], m2[1, j, 2], sides[j], solved[j])
        box_maps[0, j, :E, :E] = ww
        box_maps[0, j, E:, :E] = ew
        box_maps[0, j, :E, E:] = jnp.transpose(ew)
        box_maps[0, j, E:, E:] = ee

    for i, (other_y, _, device) in enumerate(others):
        arrive(8 + i, 1, x * 4 + other_y, device)
        arrive(11 + i, 1, (1 - x) * 4 + other_y, device)
    arrive(0, 0, partner_slot, partner)
    for i, (other_y, _, _) in enumerate(others):
        arrive(4 + i, 0, (1 - x) * 4 + other_y, partner)
    for copy in keeps:
        copy.wait()
    for copy in sends:
        copy.wait_send()
    for q in range(4):
        @pl.when(y != q)
        def _(q=q):
            share(q).wait_send()


def body(traces, leaf_maps, decap_mask):
    size_x, size_y = lax.axis_size("gx"), lax.axis_size("gy")
    dma = pltpu.SemaphoreType.DMA
    return pl.pallas_call(
        functools.partial(kernel, size_x, size_y),
        out_shape=(
            jax.ShapeDtypeStruct((1, 2, 2 * E, 2 * E), F32),
            jax.ShapeDtypeStruct((1, 2, 2 * E, K), F32),
        ),
        in_specs=[
            pl.BlockSpec(memory_space=pltpu.SMEM),
            pl.BlockSpec(memory_space=pl.ANY),
            pl.BlockSpec(memory_space=pl.ANY),
        ],
        out_specs=(pl.BlockSpec(memory_space=pltpu.VMEM), pl.BlockSpec(memory_space=pl.ANY)),
        scratch_shapes=[
            pltpu.VMEM((2, 2 * E, 4 * E), F32),
            pltpu.VMEM((2, 4, E, K), F32),
            pltpu.VMEM((2, 3, 2, E, E), F32),
            pltpu.VMEM((4, 3, 2, E, E), F32),
            pltpu.VMEM((2 * E, E), F32),
            pltpu.VMEM((2, 2, E, 512), F32),
            pltpu.VMEM((2, 2, E, 512), F32),
            pltpu.VMEM((E, K), F32),
            pltpu.VMEM((E, K), F32),
            pltpu.VMEM((2, 2 * E, E), F32),
            pltpu.VMEM((2, 2 * E, 2 * E), F32),
            pltpu.VMEM((2, 2 * E, 4 * E), BF16),
            pltpu.VMEM((2, 2 * E, 4 * E), BF16),
            pltpu.VMEM((8, 2, 2 * E, E), F32),
            pltpu.VMEM((4, 2, 2 * E, E), F32),
            pltpu.VMEM((4, 2, 2 * E, E), F32),
            pltpu.VMEM((4, 2, 2 * E, E), F32),
            pltpu.VMEM((2, 2, 2 * E, E), F32),
            pltpu.VMEM((2, 2, 3, E, E), F32),
            pltpu.VMEM((2, 2 * E, E), F32),
            pltpu.VMEM((2, 8, 2 * E, E), F32),
            dma((3,)), dma((6,)), dma((6,)), dma((3,)), dma((3,)), dma((3, 4)), dma((3, 4)),
            dma((4,)), dma((4,)), dma((4,)), dma((4,)), dma((14,)), dma((2, 8)), dma((2, 8)),
        ],
        compiler_params=pltpu.CompilerParams(
            collective_id=0, has_side_effects=True, vmem_limit_bytes=60 * 1024 * 1024
        ),
    )(decap_mask, traces, leaf_maps)


def solution(mesh):
    placed = (P("gx", "gy", None, None, None), P("gx", "gy", None, None), P("gx", "gy", None, None))
    return jax.shard_map(
        body,
        mesh=mesh,
        in_specs=placed,
        out_specs=(P("gx", "gy", None, None), P("gx", "gy", None, None)),
        check_vma=False,
    )
```
